256 devices in a mesh: wide: 32 (over z, x), narrow: 8 (over y, core).
Axes of the slice: x: 4, y: 4, z: 8, core: 2. Of those that a mesh axis runs over, the one named last changes fastest.
Arguments:
- data: bfloat16 [65536, 16384], P(('wide', 'narrow')), may hold values from -54 to 54, as said below
- players: float32 [64, 16384], P('narrow', 'wide'), may hold values from -0.046875 to 0.046875
Outputs:
- rescaled: float32 [64, 16384], P('narrow', 'wide')
The draws below stay inside these ranges and needn't reach their ends.
Inputs may be any that keep to these rules, and one draw needn't show every extreme that they name: data rows with feature and row scales of their own.
All inputs are finite; a program needn't handle non-finite values.
Results may differ from the reference program's by a relative error of at most 0.012.
Values may be sent and summed in bfloat16 or wider, within the bound.
A program may use at most 64 MiB of HBM per device.

```python
import math
import jax
import jax.numpy as jnp
from jax import lax

D = 16384
STEPS = 3
K = 64
NROWS = 65536


def draw_data(key, part):
    key = jax.random.fold_in(key, 11)
    key_base, key_cols, key_rows = jax.random.split(key, 3)
    col_scale = jnp.exp(jax.random.uniform(key_cols, (1, D), jnp.float32, math.log(0.3), math.log(3.0)))
    row_scale = jnp.exp(jax.random.uniform(key_rows, (NROWS, 1), jnp.float32, 0.0, math.log(3.0)))
    base = jnp.clip(jax.random.normal(key_base, (NROWS, D), jnp.float32), -6.0, 6.0)
    values = base * row_scale * col_scale
    return values.astype(jnp.bfloat16)


def level_of(own_key, shape, cuts, low, high):
    def one(dim, blocks):
        draws = jax.random.uniform(jax.random.fold_in(jax.random.fold_in(own_key, 6), dim), (blocks,), jnp.float32, low / len(cuts), high / len(cuts))
        return jnp.repeat(jnp.exp(draws), shape[dim] // blocks).reshape((-1,) + (1,) * (len(shape) - dim - 1))

    gain = one(*cuts[0])
    for cut in cuts[1:]:
        gain = gain * one(*cut)
    return gain


def noise(stream_key, extent, width, most, cuts=(), held_as=jnp.bfloat16):
    array = width * jax.random.normal(stream_key, extent, jnp.float32)
    if cuts:
        array = array * level_of(stream_key, extent, cuts, -0.22, 0.18)
    return jnp.clip(array, -most, most).astype(held_as)


def setup_inputs(seed: int = 0) -> dict:
    key_list = jax.random.split(jax.random.key(seed), 3)
    data = draw_data(jax.random.fold_in(key_list[2], 71), 0)
    players = noise(key_list[1], (K, D), D ** -0.5, 0.046875, ((0, 8), (1, 32)), jnp.float32)
    return {"data": data, "players": players}


step_size = 0.5
epsilon = 1e-06

def reference(data, players):
    count = K
    later = jnp.arange(count)[None, :] < jnp.arange(count)[:, None]
    v = players
    for step in range(STEPS):
        low = v.astype(jnp.bfloat16)
        proj = lax.dot_general(data, low, (((1,), (1,)), ((), ())), preferred_element_type=jnp.float32).astype(jnp.bfloat16)
        moved = lax.dot_general(proj, data, (((0,), (0,)), ((), ())), preferred_element_type=jnp.float32) / jnp.float32(NROWS)
        gram = lax.dot_general(moved, v, (((1,), (1,)), ((), ())), precision=lax.Precision.HIGHEST)
        weights = jnp.where(later, gram, jnp.float32(0.0))
        delta = moved - jnp.dot(weights, v, precision=lax.Precision.HIGHEST)
        align = lax.optimization_barrier(jnp.sum(v * delta, axis=1, keepdims=True))
        rie = delta - align * v
        upd = v + step_size * rie
        v = upd * lax.rsqrt(lax.optimization_barrier(jnp.sum(upd * upd, axis=1, keepdims=True)) + epsilon)
    return v * jnp.float32(D) ** 0.5
```

```python
import functools

import jax
import jax.numpy as jnp
from jax import lax
from jax.experimental import pallas as pl
from jax.experimental.pallas import tpu as pltpu
from jax.sharding import PartitionSpec as P

STEPS = 3
step_size = 0.5
epsilon = 1e-06

X = 4
Y = 4
ROWS = 16
LANES = 128

MESH = pl.DeviceIdType.MESH
F32 = jnp.float32
BF16 = jnp.bfloat16


def exact(a, b, contract=((1,), (0,))):
    return lax.dot_general(
        a, b, (contract, ((), ())), precision=lax.Precision.HIGHEST, preferred_element_type=F32
    )


def nt(a, b):
    return lax.dot_general(a, b, (((1,), (1,)), ((), ())), preferred_element_type=F32)


def kernel(
    Z,
    nrows,
    data_hbm,
    players_ref,
    out_ref,
    data_v,
    basis,
    pair_send,
    pair_recv,
    own,
    s1_send,
    s1a_recv,
    s1b_recv,
    s2_send,
    s2_recv,
    s3_send,
    s3_recv,
    players_recv,
    rows_v,
    data_sem,
    send_sem,
    first_recv_sem,
    ag_recv_sem,
    ag_core_sem,
    rs_core_sem,
    rs1a_sem,
    rs1b_sem,
    rs2_sem,
    rs3_sem,
):
    wide = lax.axis_index("wide")
    narrow = lax.axis_index("narrow")
    z, x = wide // X, wide % X
    y, c = narrow // 2, narrow % 2
    o = 1 - c
    count = Y * ROWS
    span = Z * LANES
    depth = data_v.shape[0]

    def at_x(d):
        return (z * X + lax.rem(x + d, X), narrow)

    def at_y(d):
        return (wide, lax.rem(y + d, Y) * 2 + c)

    def at_z(d):
        return (lax.rem(z + d, Z) * X + x, narrow)

    sibling = (wide, y * 2 + o)

    def xlanes(xq):
        return pl.ds(pl.multiple_of(xq * span, span), span)

    def yrows(yq):
        return pl.ds(pl.multiple_of(yq * ROWS, ROWS), ROWS)

    def zlanes(zq):
        return pl.ds(pl.multiple_of(zq * LANES, LANES), LANES)

    def lanes(xq, zq):
        return pl.ds(pl.multiple_of((xq * Z + zq) * LANES, LANES), LANES)

    def columns(xq, zq, cq):
        return pl.ds(pl.multiple_of(((zq * X + xq) * 2 + cq) * 2 * LANES, 2 * LANES), 2 * LANES)

    pending = []

    def send(src, dst, ssem, rsem, where):
        copy = pltpu.make_async_remote_copy(
            src_ref=src, dst_ref=dst, send_sem=ssem, recv_sem=rsem, device_id=where, device_id_type=MESH
        )
        copy.start()
        return copy

    def wait_for(ref, sem):
        pltpu.make_async_copy(ref, ref, sem).wait()

    load = pltpu.make_async_copy(data_hbm, data_v, data_sem)
    load.start()

    barrier = pltpu.get_barrier_semaphore()
    peers = [sibling]
    peers += [at_x(d) for d in range(1, X)]
    peers += [at_y(d) for d in range(1, Y)]
    peers += [at_z(d) for d in range(1, Z)]
    for peer in peers:
        pl.semaphore_signal(barrier, inc=1, device_id=peer, device_id_type=MESH)
    pl.semaphore_wait(barrier, len(peers))

    first = send(
        players_ref.at[:, pl.ds(pl.multiple_of(o * 2 * LANES, 2 * LANES), 2 * LANES)],
        players_recv,
        send_sem.at[0],
        first_recv_sem,
        sibling,
    )
    first.wait()
    mine = players_ref[:, pl.ds(pl.multiple_of(c * 2 * LANES, 2 * LANES), 2 * LANES)]
    theirs = players_recv[...]
    block = jnp.where(
        c == 0, jnp.concatenate([mine, theirs], axis=0), jnp.concatenate([theirs, mine], axis=0)
    ).astype(BF16)
    for p in range(2):
        basis[0, c, p, yrows(y), lanes(x, z)] = block[:, p * LANES : (p + 1) * LANES]

    def gather(j):
        sem = ag_recv_sem.at[j]
        for d in range(1, Z):
            part = basis.at[j, c, :, yrows(y), lanes(x, z)]
            send(part, part, send_sem.at[1], sem.at[0], at_z(d))
        got = basis.at[j, c, :, pl.ds(0, ROWS), pl.ds(0, (Z - 1) * LANES)]
        wait_for(got, sem.at[0])
        wait_for(got, send_sem.at[1])

        a2 = basis.at[j, c, 0, yrows(y), xlanes(x)]
        b2 = basis.at[j, c, 1, yrows(y), xlanes(x)]
        for d in range(1, Y):
            send(a2, a2, send_sem.at[1], sem.at[1], at_y(d))
        for d in range(1, X):
            send(b2, b2, send_sem.at[2], sem.at[2], at_x(d))
        got = basis.at[j, c, 0, pl.ds(0, (Y - 1) * ROWS), pl.ds(0, span)]
        wait_for(got, sem.at[1])
        a3 = basis.at[j, c, 0, :, xlanes(x)]
        for d in range(1, X):
            send(a3, a3, send_sem.at[3], sem.at[2 + d], at_x(d))
        got = basis.at[j, c, 0, pl.ds(0, ROWS), pl.ds(0, (X - 1) * span)]
        wait_for(got, sem.at[2])
        b3 = basis.at[j, c, 1, yrows(y), :]
        for d in range(1, Y):
            send(b3, b3, send_sem.at[4], sem.at[1 + X + d], at_y(d))
        core = ag_core_sem.at[j]
        send(a3, a3, send_sem.at[5], core.at[0], sibling)
        send(b3, b3, send_sem.at[5], core.at[0], sibling)
        order = [1] + [d for d in range(3, max(X, Y))] + [2]
        for d in order:
            if d < X:
                a = basis.at[j, c, 0, :, xlanes(lax.rem(x - d + X, X))]
                wait_for(a, sem.at[2 + d])
                send(a, a, send_sem.at[5], core.at[0], sibling)
            if d < Y:
                b = basis.at[j, c, 1, yrows(lax.rem(y - d + Y, Y)), :]
                wait_for(b, sem.at[1 + X + d])
                send(b, b, send_sem.at[5], core.at[0], sibling)

    def gather_sent(j):
        wait_for(basis.at[j, c, 0, pl.ds(0, (Y - 1) * ROWS), pl.ds(0, span)], send_sem.at[1])
        wait_for(basis.at[j, c, 0, pl.ds(0, ROWS), pl.ds(0, (X - 1) * span)], send_sem.at[2])
        wait_for(basis.at[j, c, 0, :, pl.ds(0, (X - 1) * span)], send_sem.at[3])
        wait_for(basis.at[j, c, 1, pl.ds(0, (Y - 1) * ROWS), :], send_sem.at[4])
        wait_for(basis.at[j, c], send_sem.at[5])

    def contract(j, with_data):
        def half(cq, total):
            def body(zq, total):
                q, g = total
                for xq in range(X):
                    at = lanes(xq, zq)
                    left = jnp.concatenate([basis[j, cq, 0, :, at], basis[j, cq, 1, :, at]], axis=1)
                    if with_data:
                        q = q + nt(left, data_v[:, columns(xq, zq, cq)])
                    others = [
                        jnp.concatenate([basis[b, cq, 0, :, at], basis[b, cq, 1, :, at]], axis=1)
                        for b in range(j)
                    ] + [left]
                    g = g + nt(left, jnp.concatenate(others, axis=0) if j else left)
                return q, g

            return lax.fori_loop(0, Z, body, total)

        q = jnp.zeros((count, depth if with_data else LANES), F32)
        g = jnp.zeros((count, count * (j + 1)), F32)
        total = half(c, (q, g))
        wait_for(basis.at[j, o], ag_core_sem.at[j, 0])
        q, g = half(o, total)
        return q, [g[:, b * count : (b + 1) * count] for b in range(j + 1)]

    def reduce(k, pt):
        def piece(cq, xq, store):
            def body(zq, carry):
                r = jnp.dot(pt, data_v[:, columns(xq, zq, cq)], preferred_element_type=F32)
                store(zq, r)
                return carry

            lax.fori_loop(0, Z, body, 0, unroll=min(Z, 4))

        def compute(i):
            xq = lax.rem(x + 1 + i, X)

            def to_sibling(zq, r):
                for p in range(2):
                    pair_send[i, p, :, zlanes(zq)] = r[:, p * LANES : (p + 1) * LANES].astype(BF16)

            piece(o, xq, to_sibling)
            send(pair_send.at[i], pair_recv.at[i], send_sem.at[1], rs_core_sem.at[k, i], sibling)

            def keep(zq, r):
                for p in range(2):
                    own[i, p, :, zlanes(zq)] = r[:, p * LANES : (p + 1) * LANES]

            piece(c, xq, keep)

        def spread(i):
            xq = lax.rem(x + 1 + i, X)
            wait_for(pair_recv.at[i], rs_core_sem.at[k, i])
            both = own[i] + pair_recv[i].astype(F32)
            own[i] = both
            s1_send[i] = both.astype(BF16)
            if i < X - 1:
                d = i + 1
                send(
                    s1_send.at[i, 0], s1a_recv.at[d - 1], send_sem.at[2], rs1a_sem.at[k, d - 1], at_x(d)
                )
            for d in range(1, Y):
                send(
                    s1_send.at[i, 1, yrows(lax.rem(y + d, Y)), :],
                    s1b_recv.at[i, d - 1],
                    send_sem.at[3],
                    rs1b_sem.at[k, i],
                    at_y(d),
                )

        for i in range(X):
            compute(i)
            if i:
                spread(i - 1)
        spread(X - 1)

        for d in range(1, X):
            wait_for(s1a_recv.at[d - 1], rs1a_sem.at[k, d - 1])
        total = own[X - 1, 0]
        for d in range(1, X):
            total = total + s1a_recv[d - 1].astype(F32)
        own[X - 1, 0] = total
        s2_send[0] = total.astype(BF16)
        for d in range(1, Y):
            send(
                s2_send.at[0, yrows(lax.rem(y + d, Y)), :],
                s2_recv.at[0, d - 1],
                send_sem.at[4],
                rs2_sem.at[k, 0],
                at_y(d),
            )
        for i in range(X):
            wait_for(s1b_recv.at[i], rs1b_sem.at[k, i])
            total = own[i, 1, yrows(y), :]
            for d in range(1, Y):
                total = total + s1b_recv[i, d - 1].astype(F32)
            if i < X - 1:
                s2_send[1, pl.ds(i * ROWS, ROWS), :] = total.astype(BF16)
                send(
                    s2_send.at[1, pl.ds(i * ROWS, ROWS), :],
                    s2_recv.at[1, i],
                    send_sem.at[5],
                    rs2_sem.at[k, 1],
                    at_x(i + 1),
                )
        mine_b = total

        wait_for(s2_recv.at[0], rs2_sem.at[k, 0])
        total = own[X - 1, 0, yrows(y), :]
        for d in range(1, Y):
            total = total + s2_recv[0, d - 1].astype(F32)
        own[0, 0, pl.ds(0, ROWS), :] = total
        s3_send[0] = total.astype(BF16)
        wait_for(s2_recv.at[1], rs2_sem.at[k, 1])
        total = mine_b
        for d in range(1, X):
            total = total + s2_recv[1, d - 1].astype(F32)
        own[0, 1, pl.ds(0, ROWS), :] = total
        s3_send[1] = total.astype(BF16)
        for d in range(1, Z):
            send(
                s3_send.at[:, :, zlanes(lax.rem(z + d, Z))],
                s3_recv.at[d - 1],
                send_sem.at[6],
                rs3_sem.at[k],
                at_z(d),
            )
        wait_for(s3_recv, rs3_sem.at[k])
        total = own[0, :, pl.ds(0, ROWS), zlanes(z)]
        for d in range(1, Z):
            total = total + s3_recv[d - 1].astype(F32)
        basis[k + 1, c, :, yrows(y), lanes(x, z)] = total.astype(BF16)

        wait_for(pair_send, send_sem.at[1])
        wait_for(s1a_recv, send_sem.at[2])
        wait_for(s1b_recv, send_sem.at[3])
        wait_for(s2_recv.at[0], send_sem.at[4])
        wait_for(s2_recv.at[1], send_sem.at[5])
        wait_for(s3_recv, send_sem.at[6])

    row = lax.broadcasted_iota(jnp.int32, (count, count), 0)
    col = lax.broadcasted_iota(jnp.int32, (count, count), 1)
    eye = jnp.where(row == col, F32(1.0), F32(0.0))

    gather(0)
    load.wait()
    proj, (gvv,) = contract(0, True)
    coef = [eye]
    gather_sent(0)

    for k in range(STEPS):
        reduce(k, (proj.astype(BF16).astype(F32) * F32(1.0 / nrows)).astype(BF16))
        gather(k + 1)
        q, inner = contract(k + 1, k + 1 < STEPS)
        gram = exact(inner[0], coef[0], ((1,), (1,)))
        for b in range(1, k + 1):
            gram = gram + exact(inner[b], coef[b], ((1,), (1,)))
        weights = jnp.where(col < row, gram, F32(0.0))
        align = jnp.sum(eye * gram - weights * gvv, axis=1, keepdims=True)
        mix = eye * (F32(1.0) - F32(step_size) * align) - F32(step_size) * weights
        mixed = exact(mix, gvv)
        length = jnp.sum(
            mixed * mix + F32(2 * step_size) * mix * gram + F32(step_size**2) * eye * inner[k + 1],
            axis=1,
            keepdims=True,
        )
        scale = lax.rsqrt(length + F32(epsilon))
        if k + 1 < STEPS:
            proj = scale * (exact(mix, proj) + F32(step_size) * q)
            cross = exact(mix, gram, ((1,), (1,)))
            guu = (
                exact(mixed, mix, ((1,), (1,)))
                + F32(step_size) * (cross + cross.T)
                + F32(step_size**2) * inner[k + 1]
            )
            gvv = scale * guu * jnp.sum(eye * scale, axis=0, keepdims=True)
        coef = [scale * exact(mix, a) for a in coef] + [scale * F32(step_size) * eye]
        gather_sent(k + 1)

    at = lanes(x, z)
    total = jnp.zeros((count, 4 * LANES), F32)
    for b in range(STEPS + 1):
        wide_rows = jnp.concatenate(
            [basis[b, cq, p, :, at] for cq in range(2) for p in range(2)], axis=1
        ).astype(F32)
        total = total + exact(coef[b], wide_rows)
    rows_v[...] = total
    features = X * Z * 4 * LANES
    out_ref[...] = rows_v[pl.ds(pl.multiple_of(narrow * (ROWS // 2), ROWS // 2), ROWS // 2), :] * F32(
        features**0.5
    )


def on_device(data, players):
    Z = lax.axis_size("wide") // X
    depth, features = data.shape
    nrows = depth * lax.axis_size("wide") * lax.axis_size("narrow")
    count = Y * ROWS
    span = Z * LANES
    dma = pltpu.SemaphoreType.DMA
    flops = STEPS * 4 * count * features * depth
    return pl.pallas_call(
        functools.partial(kernel, Z, nrows),
        out_shape=jax.ShapeDtypeStruct(players.shape, F32),
        in_specs=[pl.BlockSpec(memory_space=pl.ANY), pl.BlockSpec(memory_space=pltpu.VMEM)],
        out_specs=pl.BlockSpec(memory_space=pltpu.VMEM),
        scratch_shapes=[
            pltpu.VMEM((depth, features), BF16),
            pltpu.VMEM((STEPS + 1, 2, 2, count, X * span), BF16),
            pltpu.VMEM((X, 2, count, span), BF16),
            pltpu.VMEM((X, 2, count, span), BF16),
            pltpu.VMEM((X, 2, count, span), F32),
            pltpu.VMEM((X, 2, count, span), BF16),
            pltpu.VMEM((X - 1, count, span), BF16),
            pltpu.VMEM((X, Y - 1, ROWS, span), BF16),
            pltpu.VMEM((2, count, span), BF16),
            pltpu.VMEM((2, max(X, Y) - 1, ROWS, span), BF16),
            pltpu.VMEM((2, ROWS, span), BF16),
            pltpu.VMEM((Z - 1, 2, ROWS, LANES), BF16),
            pltpu.VMEM((ROWS // 2, 2 * LANES), F32),
            pltpu.VMEM((count, 4 * LANES), F32),
            dma,
            dma((7,)),
            dma,
            dma((STEPS + 1, 1 + X + Y)),
            dma((STEPS + 1, 1)),
            dma((STEPS, X)),
            dma((STEPS, X - 1)),
            dma((STEPS, X)),
            dma((STEPS, 2)),
            dma((STEPS,)),
        ],
        compiler_params=pltpu.CompilerParams(
            collective_id=0, has_side_effects=True, vmem_limit_bytes=52 * 2**20
        ),
        cost_estimate=pl.CostEstimate(flops=flops, bytes_accessed=2 * depth * features, transcendentals=0),
    )(data, players)


def solution(mesh):
    placed = (P(("wide", "narrow"), None), P("narrow", "wide"))
    return jax.shard_map(
        on_device, mesh=mesh, in_specs=placed, out_specs=P("narrow", "wide"), check_vma=False
    )
```

```python
import functools

import jax
import jax.numpy as jnp
from jax import lax
from jax.experimental import pallas as pl
from jax.experimental.pallas import tpu as pltpu
from jax.sharding import PartitionSpec as P

STEPS = 3
step_size = 0.5
epsilon = 1e-06

X = 4
Y = 4
ROWS = 16
HALF = ROWS // 2
LANES = 256
UNITS = 4

MESH = pl.DeviceIdType.MESH
F32 = jnp.float32
BF16 = jnp.bfloat16


def exact(a, b, contract=((1,), (0,))):
    return lax.dot_general(
        a, b, (contract, ((), ())), precision=lax.Precision.HIGHEST, preferred_element_type=F32
    )


def nt(a, b):
    return lax.dot_general(a, b, (((1,), (1,)), ((), ())), preferred_element_type=F32)


def kernel(
    Z,
    nrows,
    data_hbm,
    players_ref,
    out_ref,
    data_v,
    basis,
    players_recv,
    part_send,
    part_recv,
    s1_send,
    s1_recv,
    s2_send,
    s2_recv,
    s2_own,
    s3_send,
    z_recv,
    last_recv,
    gram_send,
    gram_recv,
    gram_z_recv,
    sq_send,
    sq_recv,
    sq_z_recv,
    sq_core_recv,
    upd_v,
    upd_recv,
    gvv_v,
    load_sem,
    swap_send_sem,
    swap_recv_sem,
    send_sem,
    first_sem,
    part_sem,
    z0_sem,
    s1_sem,
    s2_sem,
    s3_sem,
    s4_sem,
    s5_sem,
    gram_sem,
    sq_sem,
    upd_sem,
):
    U = min(UNITS, Z)
    zpu = Z // U
    wide = lax.axis_index("wide")
    narrow = lax.axis_index("narrow")
    z, x = wide // X, wide % X
    y, c = narrow // 2, narrow % 2
    o = 1 - c
    count = Y * ROWS
    span = zpu * LANES
    unit = X * span
    depth = data_hbm.shape[0]

    def at_x(d):
        return (z * X + lax.rem(x + d, X), narrow)

    def at_y(d):
        return (wide, lax.rem(y + d, Y) * 2 + c)

    def at_z(d):
        return (lax.rem(z + d, Z) * X + x, narrow)

    sibling = (wide, y * 2 + o)

    def piece(at, size):
        return pl.ds(pl.multiple_of(at * size, size), size)

    def send(src, dst, ssem, rsem, where):
        pltpu.make_async_remote_copy(
            src_ref=src, dst_ref=dst, send_sem=ssem, recv_sem=rsem, device_id=where, device_id_type=MESH
        ).start()

    def wait_for(ref, sem):
        pltpu.make_async_copy(ref, ref, sem).wait()

    barrier = pltpu.get_barrier_semaphore()
    peers = [sibling]
    peers += [at_x(d) for d in range(1, X)]
    peers += [at_y(d) for d in range(1, Y)]
    peers += [at_z(d) for d in range(1, Z)]
    for peer in peers:
        pl.semaphore_signal(barrier, inc=1, device_id=peer, device_id_type=MESH)
    pl.semaphore_wait(barrier, len(peers))

    send(players_ref.at[:, piece(o, LANES)], players_recv, send_sem.at[0], first_sem, sibling)

    def swap(q, carry):
        zq, xq = q // X, lax.rem(q, X)
        to = piece(((zq // zpu) * X + xq) * zpu + lax.rem(zq, zpu), LANES)
        rows = piece(c, depth)
        pltpu.make_async_copy(data_hbm.at[:, piece(q * 2 + c, LANES)], data_v.at[rows, to], load_sem).start()
        send(
            data_hbm.at[:, piece(q * 2 + o, LANES)], data_v.at[rows, to], swap_send_sem, swap_recv_sem, sibling
        )
        return carry

    lax.fori_loop(0, Z * X, swap, 0)

    wait_for(players_recv, first_sem)
    mine = players_ref[:, piece(c, LANES)]
    theirs = players_recv[...]
    my_block = (z // zpu, pl.ds(pl.multiple_of(y * ROWS, ROWS), ROWS), piece(x * zpu + lax.rem(z, zpu), LANES))
    basis[(0, *my_block)] = jnp.where(
        c == 0, jnp.concatenate([mine, theirs], axis=0), jnp.concatenate([theirs, mine], axis=0)
    ).astype(BF16)
    for d in range(1, Z):
        part = basis.at[(0, *my_block)]
        send(part, part, send_sem.at[1], z0_sem, at_z(d))

    def fourth(j, u):
        part = basis.at[j, u, piece(y, ROWS), piece(x, span)]
        if u % 2 == 0:
            for d in range(1, Y):
                send(part, part, send_sem.at[2], s4_sem.at[j, u], at_y(d))
        else:
            for d in range(1, X):
                send(part, part, send_sem.at[2], s4_sem.at[j, u], at_x(d))

    def fifth(j, u):
        if u % 2 == 0:
            wait_for(s2_recv.at[u, pl.ds(0, Y - 1)], s4_sem.at[j, u])
            part = basis.at[j, u, :, piece(x, span)]
            for d in range(1, X):
                send(part, part, send_sem.at[3], s5_sem.at[j, u], at_x(d))
        else:
            wait_for(s2_recv.at[u, pl.ds(0, X - 1)], s4_sem.at[j, u])
            part = basis.at[j, u, piece(y, ROWS), :]
            for d in range(1, Y):
                send(part, part, send_sem.at[3], s5_sem.at[j, u], at_y(d))

    def contract(j, u):
        if u % 2 == 0:
            wait_for(basis.at[j, u, :, pl.ds(0, (X - 1) * span)], s5_sem.at[j, u])
        else:
            wait_for(basis.at[j, u, pl.ds(0, (Y - 1) * ROWS), :], s5_sem.at[j, u])
        if j == 0 and u == 0:
            wait_for(data_v.at[pl.ds(0, depth)], load_sem)
            wait_for(data_v.at[pl.ds(0, depth)], swap_recv_sem)
        left = basis[j, u]
        q = nt(left, data_v[:, u * unit : (u + 1) * unit])
        g = jnp.concatenate([nt(left, basis[b, u]) for b in range(j + 1)], axis=1)
        if u == 0:
            part_send[j, :, : 2 * depth] = q
            part_send[j, :, 2 * depth : 2 * depth + (j + 1) * count] = g
        else:
            part_send[j, :, : 2 * depth] += q
            part_send[j, :, 2 * depth : 2 * depth + (j + 1) * count] += g

    def whole(j):
        part = part_send.at[j]
        send(part, part_recv.at[j], send_sem.at[4], part_sem.at[j], sibling)
        wait_for(part, part_sem.at[j])
        total = part_send[j, :, : 2 * depth + (j + 1) * count] + part_recv[j, :, : 2 * depth + (j + 1) * count]
        return total[:, : 2 * depth], [
            total[:, 2 * depth + b * count : 2 * depth + (b + 1) * count] for b in range(j + 1)
        ]

    def gather_sent(j):
        for u in range(U):
            peers4, peers5 = (Y - 1, X - 1) if u % 2 == 0 else (X - 1, Y - 1)
            wait_for(s2_recv.at[u, pl.ds(0, peers4)], send_sem.at[2])
            if u % 2 == 0:
                wait_for(basis.at[j, u, :, pl.ds(0, (X - 1) * span)], send_sem.at[3])
            else:
                wait_for(basis.at[j, u, pl.ds(0, (Y - 1) * ROWS), :], send_sem.at[3])
        wait_for(part_send.at[j], send_sem.at[4])

    def first_stage(k, u, pt):
        for xq in range(X):
            at = u * unit + xq * span
            r = jnp.dot(pt, data_v[:, at : at + span], preferred_element_type=F32)
            s1_send[u, :, xq * span : (xq + 1) * span] = r.astype(BF16)
        if u % 2 == 0:
            for d in range(1, X):
                send(
                    s1_send.at[u, :, piece(lax.rem(x + d, X), span)],
                    s1_recv.at[u, :, pl.ds((d - 1) * span, span)],
                    send_sem.at[5],
                    s1_sem.at[k, u],
                    at_x(d),
                )
        else:
            for d in range(1, Y):
                send(
                    s1_send.at[u, piece(lax.rem(y + d, Y), ROWS), :],
                    s1_recv.at[u, pl.ds((d - 1) * ROWS, ROWS), :],
                    send_sem.at[5],
                    s1_sem.at[k, u],
                    at_y(d),
                )

    def second_stage(k, u):
        if u % 2 == 0:
            wait_for(s1_recv.at[u, :, pl.ds(0, (X - 1) * span)], s1_sem.at[k, u])
            total = s1_send[u, :, piece(x, span)].astype(F32)
            for d in range(1, X):
                total = total + s1_recv[u, :, (d - 1) * span : d * span].astype(F32)
            s2_send[u] = total.astype(BF16)
            for d in range(1, Y):
                send(
                    s2_send.at[u, piece(lax.rem(y + d, Y), ROWS), :],
                    s2_recv.at[u, d - 1],
                    send_sem.at[6],
                    s2_sem.at[k, u],
                    at_y(d),
                )
        else:
            wait_for(s1_recv.at[u, pl.ds(0, (Y - 1) * ROWS), :], s1_sem.at[k, u])
            total = s1_send[u, piece(y, ROWS), :].astype(F32)
            for d in range(1, Y):
                total = total + s1_recv[u, (d - 1) * ROWS : d * ROWS, :].astype(F32)
            for xq in range(X):
                s2_send[u, xq * ROWS : (xq + 1) * ROWS, :] = total[:, xq * span : (xq + 1) * span].astype(BF16)
            for d in range(1, X):
                send(
                    s2_send.at[u, piece(lax.rem(x + d, X), ROWS), :],
                    s2_recv.at[u, d - 1],
                    send_sem.at[6],
                    s2_sem.at[k, u],
                    at_x(d),
                )

    def plane_sum(k, u):
        n = Y if u % 2 == 0 else X
        wait_for(s2_recv.at[u, pl.ds(0, n - 1)], s2_sem.at[k, u])
        total = s2_send[u, piece(y if u % 2 == 0 else x, ROWS), :].astype(F32)
        for d in range(1, n):
            total = total + s2_recv[u, d - 1].astype(F32)
        return total

    def third_stage(k, u):
        total = plane_sum(k, u)
        s2_own[u] = total
        s3_send[u] = total.astype(BF16)
        for d in range(1, Z):
            send(s3_send.at[u], z_recv.at[k, u, d - 1], send_sem.at[7], s3_sem.at[k, u], at_z(d))

    def rows_done(k, u):
        wait_for(z_recv.at[k, u], s3_sem.at[k, u])
        total = s2_own[u]
        for d in range(1, Z):
            total = total + z_recv[k, u, d - 1].astype(F32)
        basis[k + 1, u, piece(y, ROWS), piece(x, span)] = total.astype(BF16)
        fourth(k + 1, u)

    def reduce_sent(k):
        for u in range(U):
            if u % 2 == 0:
                wait_for(s1_recv.at[u, :, pl.ds(0, (X - 1) * span)], send_sem.at[5])
                wait_for(s2_recv.at[u, pl.ds(0, Y - 1)], send_sem.at[6])
            else:
                wait_for(s1_recv.at[u, pl.ds(0, (Y - 1) * ROWS), :], send_sem.at[5])
                wait_for(s2_recv.at[u, pl.ds(0, X - 1)], send_sem.at[6])

    row = lax.broadcasted_iota(jnp.int32, (count, count), 0)
    col = lax.broadcasted_iota(jnp.int32, (count, count), 1)
    eye = jnp.where(row == col, F32(1.0), F32(0.0))

    def weigh(gram, gvv, lower, diagonal):
        weights = jnp.where(lower, gram, F32(0.0))
        align = jnp.sum(diagonal * gram - weights * gvv, axis=1, keepdims=True)
        return diagonal * (F32(1.0) - F32(step_size) * align) - F32(step_size) * weights

    wait_for(z_recv.at[0, 0, :, :, pl.ds(0, LANES)], z0_sem)
    for u in range(U):
        fourth(0, u)
    for u in range(U):
        fifth(0, u)
    for u in range(U):
        contract(0, u)
    proj, (gvv,) = whole(0)
    coef = [eye]
    wait_for(players_recv, send_sem.at[0])
    wait_for(z_recv.at[0, 0, :, :, pl.ds(0, LANES)], send_sem.at[1])
    wait_for(data_v.at[pl.ds(0, depth)], swap_send_sem)

    for k in range(STEPS - 1):
        pt = (proj.astype(BF16).astype(F32) * F32(1.0 / nrows)).astype(BF16)
        for u in range(U):
            first_stage(k, u, pt)
        gather_sent(k)
        for u in range(U):
            second_stage(k, u)
        for u in range(U):
            third_stage(k, u)
        for u in range(U):
            rows_done(k, u)
        for u in range(U):
            fifth(k + 1, u)
        for u in range(U):
            contract(k + 1, u)
        q, inner = whole(k + 1)
        gram = exact(inner[0], coef[0], ((1,), (1,)))
        for b in range(1, k + 1):
            gram = gram + exact(inner[b], coef[b], ((1,), (1,)))
        mix = weigh(gram, gvv, col < row, eye)
        mixed = exact(mix, gvv)
        length = jnp.sum(
            mixed * mix + F32(2 * step_size) * mix * gram + F32(step_size**2) * eye * inner[k + 1],
            axis=1,
            keepdims=True,
        )
        scale = lax.rsqrt(length + F32(epsilon))
        proj = scale * (exact(mix, proj) + F32(step_size) * q)
        cross = exact(mix, gram, ((1,), (1,)))
        guu = (
            exact(mixed, mix, ((1,), (1,)))
            + F32(step_size) * (cross + cross.T)
            + F32(step_size**2) * inner[k + 1]
        )
        gvv = scale * guu * jnp.sum(eye * scale, axis=0, keepdims=True)
        coef = [scale * exact(mix, a) for a in coef] + [scale * F32(step_size) * eye]
        reduce_sent(k)
        wait_for(z_recv.at[k], send_sem.at[7])

    k = STEPS - 1
    pt = (proj.astype(BF16).astype(F32) * F32(1.0 / nrows)).astype(BF16)
    gram = exact(pt.astype(F32), proj, ((1,), (1,)))
    gram_send[0] = jnp.concatenate([gram, jnp.zeros((count, 128 - count), F32)], axis=1)
    for d in range(1, Y):
        send(
            gram_send.at[0, piece(lax.rem(y + d, Y), ROWS), :],
            gram_recv.at[0, d - 1],
            send_sem.at[8],
            gram_sem.at[0],
            at_y(d),
        )
    for u in range(U):
        first_stage(k, u, pt)
    gather_sent(k)
    wait_for(gram_recv.at[0, pl.ds(0, Y - 1)], gram_sem.at[0])
    total = gram_send[0, piece(y, ROWS), :]
    for d in range(1, Y):
        total = total + gram_recv[0, d - 1]
    gram_send[1, :ROWS, :] = total
    for d in range(1, X):
        send(
            gram_send.at[1, pl.ds(0, ROWS)], gram_recv.at[1, d - 1], send_sem.at[9], gram_sem.at[1], at_x(d)
        )
    for u in range(U):
        second_stage(k, u)
    wait_for(gram_recv.at[1, pl.ds(0, X - 1)], gram_sem.at[1])
    total = gram_send[1, :ROWS, :]
    for d in range(1, X):
        total = total + gram_recv[1, d - 1]
    gram_send[2, :ROWS, :] = total
    for d in range(1, Z):
        send(
            gram_send.at[2, pl.ds(0, ROWS)], gram_z_recv.at[d - 1], send_sem.at[10], gram_sem.at[2], at_z(d)
        )
    for u in range(U):
        total = plane_sum(k, u)
        s2_own[u] = total
        s3_send[u] = total.astype(BF16)
    for d in range(1, Z):
        zq = lax.rem(z + d, Z)
        send(
            s3_send.at[zq // zpu, :, piece(lax.rem(zq, zpu), LANES)],
            last_recv.at[d - 1],
            send_sem.at[7],
            s3_sem.at[k, 0],
            at_z(d),
        )
    v = jnp.zeros((count, LANES), F32)
    for b in range(STEPS):
        v = v + exact(coef[b], basis[b, z // zpu, :, piece(x * zpu + lax.rem(z, zpu), LANES)].astype(F32))
    gvv_v[...] = gvv
    row = lax.broadcasted_iota(jnp.int32, (ROWS, count), 0) + y * ROWS
    col = lax.broadcasted_iota(jnp.int32, (ROWS, count), 1)
    wait_for(gram_z_recv, gram_sem.at[2])
    total = gram_send[2, :ROWS, :]
    for d in range(1, Z):
        total = total + gram_z_recv[d - 1]
    mix = weigh(
        total[:, :count], gvv_v[piece(y, ROWS), :], col < row, jnp.where(row == col, F32(1.0), F32(0.0))
    )
    upd = exact(mix, v)
    wait_for(last_recv, s3_sem.at[k, 0])
    moved = s2_own[z // zpu, :, piece(lax.rem(z, zpu), LANES)]
    for d in range(1, Z):
        moved = moved + last_recv[d - 1].astype(F32)
    upd = upd + F32(step_size) * moved
    upd_v[...] = upd
    send(upd_v.at[piece(o, HALF), :], upd_recv, send_sem.at[0], upd_sem, sibling)
    sq_send[0] = jnp.broadcast_to(jnp.sum(upd * upd, axis=1, keepdims=True), (ROWS, 128))
    for d in range(1, Z):
        send(sq_send.at[0], sq_z_recv.at[d - 1], send_sem.at[1], sq_sem.at[0], at_z(d))
    wait_for(sq_z_recv, sq_sem.at[0])
    total = sq_send[0]
    for d in range(1, Z):
        total = total + sq_z_recv[d - 1]
    sq_send[1] = total
    for d in range(1, X):
        send(sq_send.at[1], sq_recv.at[d - 1], send_sem.at[2], sq_sem.at[1], at_x(d))
    wait_for(sq_recv, sq_sem.at[1])
    total = sq_send[1]
    for d in range(1, X):
        total = total + sq_recv[d - 1]
    sq_send[2] = total
    send(sq_send.at[2], sq_core_recv, send_sem.at[3], sq_sem.at[2], sibling)
    wait_for(sq_core_recv, sq_sem.at[2])
    wait_for(upd_recv, upd_sem)
    length = (sq_send[2, piece(c, HALF), :] + sq_core_recv[piece(c, HALF), :])[:, :1]
    scale = lax.rsqrt(length + F32(epsilon)) * F32((Z * X * 2 * LANES) ** 0.5)
    out_ref[:, piece(c, LANES)] = upd_v[piece(c, HALF), :] * scale
    out_ref[:, piece(o, LANES)] = upd_recv[...] * scale

    reduce_sent(k)
    wait_for(last_recv, send_sem.at[7])
    wait_for(gram_recv.at[0, pl.ds(0, Y - 1)], send_sem.at[8])
    wait_for(gram_recv.at[1, pl.ds(0, X - 1)], send_sem.at[9])
    wait_for(gram_z_recv, send_sem.at[10])
    wait_for(upd_recv, send_sem.at[0])
    wait_for(sq_z_recv, send_sem.at[1])
    wait_for(sq_recv, send_sem.at[2])
    wait_for(sq_core_recv, send_sem.at[3])


def on_device(data, players):
    Z = lax.axis_size("wide") // X
    U = min(UNITS, Z)
    depth, features = data.shape
    nrows = depth * lax.axis_size("wide") * lax.axis_size("narrow")
    count = Y * ROWS
    span = Z // U * LANES
    most = max(X, Y) - 1
    parts = 2 * depth + STEPS * count
    parts = -(-parts // 128) * 128
    dma = pltpu.SemaphoreType.DMA
    flops = STEPS * 4 * count * features * depth
    return pl.pallas_call(
        functools.partial(kernel, Z, nrows),
        out_shape=jax.ShapeDtypeStruct(players.shape, F32),
        in_specs=[pl.BlockSpec(memory_space=pl.ANY), pl.BlockSpec(memory_space=pltpu.VMEM)],
        out_specs=pl.BlockSpec(memory_space=pltpu.VMEM),
        scratch_shapes=[
            pltpu.VMEM((2 * depth, features // 2), BF16),
            pltpu.VMEM((STEPS, U, count, X * span), BF16),
            pltpu.VMEM((HALF, LANES), F32),
            pltpu.VMEM((STEPS, count, parts), F32),
            pltpu.VMEM((STEPS, count, parts), F32),
            pltpu.VMEM((U, count, X * span), BF16),
            pltpu.VMEM((U, count, X * span), BF16),
            pltpu.VMEM((U, max(X, Y) * ROWS, span), BF16),
            pltpu.VMEM((U, most, ROWS, span), BF16),
            pltpu.VMEM((U, ROWS, span), F32),
            pltpu.VMEM((U, ROWS, span), BF16),
            pltpu.VMEM((STEPS - 1, U, Z - 1, ROWS, span), BF16),
            pltpu.VMEM((Z - 1, ROWS, LANES), BF16),
            pltpu.VMEM((3, count, 128), F32),
            pltpu.VMEM((2, most, ROWS, 128), F32),
            pltpu.VMEM((Z - 1, ROWS, 128), F32),
            pltpu.VMEM((3, ROWS, 128), F32),
            pltpu.VMEM((X - 1, ROWS, 128), F32),
            pltpu.VMEM((Z - 1, ROWS, 128), F32),
            pltpu.VMEM((ROWS, 128), F32),
            pltpu.VMEM((ROWS, LANES), F32),
            pltpu.VMEM((HALF, LANES), F32),
            pltpu.VMEM((count, count), F32),
            dma,
            dma,
            dma,
            dma((11,)),
            dma,
            dma((STEPS,)),
            dma,
            dma((STEPS, U)),
            dma((STEPS, U)),
            dma((STEPS, U)),
            dma((STEPS, U)),
            dma((STEPS, U)),
            dma((3,)),
            dma((3,)),
            dma,
        ],
        compiler_params=pltpu.CompilerParams(
            collective_id=0, has_side_effects=True, vmem_limit_bytes=52 * 2**20
        ),
        cost_estimate=pl.CostEstimate(flops=flops, bytes_accessed=2 * depth * features, transcendentals=0),
    )(data, players)


def solution(mesh):
    placed = (P(("wide", "narrow"), None), P("narrow", "wide"))
    return jax.shard_map(
        on_device, mesh=mesh, in_specs=placed, out_specs=P("narrow", "wide"), check_vma=False
    )
```

```python
import functools

import jax
import jax.numpy as jnp
from jax import lax
from jax.experimental import pallas as pl
from jax.experimental.pallas import tpu as pltpu
from jax.sharding import PartitionSpec as P

STEPS = 3
step_size = 0.5
epsilon = 1e-06

X = 4
Y = 4
ROWS = 16
HALF = ROWS // 2
LANES = 256

MESH = pl.DeviceIdType.MESH
F32 = jnp.float32
BF16 = jnp.bfloat16


def exact(a, b, contract=((1,), (0,))):
    return lax.dot_general(
        a, b, (contract, ((), ())), precision=lax.Precision.HIGHEST, preferred_element_type=F32
    )


def nt(a, b):
    return lax.dot_general(a, b, (((1,), (1,)), ((), ())), preferred_element_type=F32)


def kernel(
    Z,
    nrows,
    data_hbm,
    players_ref,
    out_ref,
    data_v,
    basis,
    players_recv,
    part_send,
    part_recv,
    s1_send,
    s1_recv,
    s2_send,
    s2_recv,
    s2_own,
    s3_send,
    z_recv,
    gram_send,
    gram_recv,
    gram_z_recv,
    sq_send,
    sq_recv,
    sq_z_recv,
    sq_core_recv,
    upd_v,
    upd_recv,
    gvv_v,
    load_sem,
    swap_send_sem,
    swap_recv_sem,
    send_sem,
    first_sem,
    part_sem,
    za_sem,
    s1_sem,
    s2_sem,
    s3_sem,
    s4_sem,
    s5_sem,
    gram_sem,
    sq_sem,
    upd_sem,
):
    wide = lax.axis_index("wide")
    narrow = lax.axis_index("narrow")
    z, x = wide // X, wide % X
    y, c = narrow // 2, narrow % 2
    o = 1 - c
    count = Y * ROWS
    span = LANES
    unit = X * span
    near = sorted(range(Z), key=lambda d: (min(d, Z - d), d))
    far = near[::-1]
    depth = data_hbm.shape[0]

    def at_x(d):
        return (z * X + lax.rem(x + d, X), narrow)

    def at_y(d):
        return (wide, lax.rem(y + d, Y) * 2 + c)

    def at_z(d):
        return (lax.rem(z + d, Z) * X + x, narrow)

    sibling = (wide, y * 2 + o)

    def piece(at, size):
        return pl.ds(pl.multiple_of(at * size, size), size)

    def send(src, dst, ssem, rsem, where):
        pltpu.make_async_remote_copy(
            src_ref=src, dst_ref=dst, send_sem=ssem, recv_sem=rsem, device_id=where, device_id_type=MESH
        ).start()

    def wait_for(ref, sem):
        pltpu.make_async_copy(ref, ref, sem).wait()

    def place(q):
        return piece(c, depth), piece(lax.rem(q // X - z + Z, Z) * X + lax.rem(q, X), LANES)

    def load(q, carry):
        pltpu.make_async_copy(data_hbm.at[:, piece(q * 2 + c, LANES)], data_v.at[place(q)], load_sem).start()
        return carry

    lax.fori_loop(0, Z * X, load, 0)

    barrier = pltpu.get_barrier_semaphore()
    peers = [sibling]
    peers += [at_x(d) for d in range(1, X)]
    peers += [at_y(d) for d in range(1, Y)]
    peers += [at_z(d) for d in range(1, Z)]
    for peer in peers:
        pl.semaphore_signal(barrier, inc=1, device_id=peer, device_id_type=MESH)
    pl.semaphore_wait(barrier, len(peers))

    send(players_ref.at[:, piece(o, LANES)], players_recv, send_sem.at[0], first_sem, sibling)

    wait_for(players_recv, first_sem)
    mine = players_ref[:, piece(c, LANES)]
    theirs = players_recv[...]
    basis[0, 0, piece(y, ROWS), piece(x, span)] = jnp.where(
        c == 0, jnp.concatenate([mine, theirs], axis=0), jnp.concatenate([theirs, mine], axis=0)
    ).astype(BF16)

    def along_z(j):
        for d in near[1:]:
            send(
                basis.at[j, 0, piece(y, ROWS), piece(x, span)],
                basis.at[j, Z - d, piece(y, ROWS), piece(x, span)],
                send_sem.at[1],
                za_sem.at[j, Z - d],
                at_z(d),
            )

    def swap(q, carry):
        send(
            data_hbm.at[:, piece(q * 2 + o, LANES)],
            data_v.at[place(q)],
            swap_send_sem,
            swap_recv_sem,
            sibling,
        )
        return carry

    def fourth(j, u):
        if u:
            wait_for(z_recv.at[0, 0], za_sem.at[j, u])
        part = basis.at[j, u, piece(y, ROWS), piece(x, span)]
        if u % 2 == 0:
            for d in range(1, Y):
                send(part, part, send_sem.at[2], s4_sem.at[j, u], at_y(d))
        else:
            for d in range(1, X):
                send(part, part, send_sem.at[2], s4_sem.at[j, u], at_x(d))

    def fifth(j, u):
        if u % 2 == 0:
            wait_for(s2_recv.at[u, pl.ds(0, Y - 1)], s4_sem.at[j, u])
            part = basis.at[j, u, :, piece(x, span)]
            for d in range(1, X):
                send(part, part, send_sem.at[3], s5_sem.at[j, u], at_x(d))
        else:
            wait_for(s2_recv.at[u, pl.ds(0, X - 1)], s4_sem.at[j, u])
            part = basis.at[j, u, piece(y, ROWS), :]
            for d in range(1, Y):
                send(part, part, send_sem.at[3], s5_sem.at[j, u], at_y(d))

    def contract(j, u):
        if u % 2 == 0:
            wait_for(basis.at[j, u, :, pl.ds(0, (X - 1) * span)], s5_sem.at[j, u])
        else:
            wait_for(basis.at[j, u, pl.ds(0, (Y - 1) * ROWS), :], s5_sem.at[j, u])
        if j == 0 and u == near[0]:
            wait_for(data_v.at[pl.ds(0, depth)], load_sem)
            wait_for(data_v.at[pl.ds(0, depth)], swap_recv_sem)
        left = basis[j, u]
        q = nt(left, data_v[:, u * unit : (u + 1) * unit])
        g = jnp.concatenate([nt(left, basis[b, u]) for b in range(j + 1)], axis=1)
        if u == near[0]:
            part_send[j, :, : 2 * depth] = q
            part_send[j, :, 2 * depth : 2 * depth + (j + 1) * count] = g
        else:
            part_send[j, :, : 2 * depth] += q
            part_send[j, :, 2 * depth : 2 * depth + (j + 1) * count] += g

    def whole(j):
        part = part_send.at[j]
        send(part, part_recv.at[j], send_sem.at[4], part_sem.at[j], sibling)
        wait_for(part, part_sem.at[j])
        total = part_send[j, :, : 2 * depth + (j + 1) * count] + part_recv[j, :, : 2 * depth + (j + 1) * count]
        return total[:, : 2 * depth], [
            total[:, 2 * depth + b * count : 2 * depth + (b + 1) * count] for b in range(j + 1)
        ]

    def gather(j):
        fourth(j, 0)
        for u in near[1:3]:
            fourth(j, u)
        fifth(j, 0)
        for u in near[3:]:
            fourth(j, u)
        for u in near[1:]:
            fifth(j, u)
        for u in near:
            contract(j, u)

    def gather_sent(j):
        wait_for(z_recv.at[0], send_sem.at[1])
        for u in range(Z):
            peers4, peers5 = (Y - 1, X - 1) if u % 2 == 0 else (X - 1, Y - 1)
            wait_for(s2_recv.at[u, pl.ds(0, peers4)], send_sem.at[2])
            if u % 2 == 0:
                wait_for(basis.at[j, u, :, pl.ds(0, (X - 1) * span)], send_sem.at[3])
            else:
                wait_for(basis.at[j, u, pl.ds(0, (Y - 1) * ROWS), :], send_sem.at[3])
        wait_for(part_send.at[j], send_sem.at[4])

    def first_stage(k, u, pt):
        for xq in range(X):
            at = u * unit + xq * span
            r = jnp.dot(pt, data_v[:, at : at + span], preferred_element_type=F32)
            s1_send[u, :, xq * span : (xq + 1) * span] = r.astype(BF16)
        if u % 2 == 0:
            for d in range(1, X):
                send(
                    s1_send.at[u, :, piece(lax.rem(x + d, X), span)],
                    s1_recv.at[u, :, pl.ds((d - 1) * span, span)],
                    send_sem.at[5],
                    s1_sem.at[k, u],
                    at_x(d),
                )
        else:
            for d in range(1, Y):
                send(
                    s1_send.at[u, piece(lax.rem(y + d, Y), ROWS), :],
                    s1_recv.at[u, pl.ds((d - 1) * ROWS, ROWS), :],
                    send_sem.at[5],
                    s1_sem.at[k, u],
                    at_y(d),
                )

    def second_stage(k, u):
        if u % 2 == 0:
            wait_for(s1_recv.at[u, :, pl.ds(0, (X - 1) * span)], s1_sem.at[k, u])
            total = s1_send[u, :, piece(x, span)].astype(F32)
            for d in range(1, X):
                total = total + s1_recv[u, :, (d - 1) * span : d * span].astype(F32)
            s2_send[u] = total.astype(BF16)
            for d in range(1, Y):
                send(
                    s2_send.at[u, piece(lax.rem(y + d, Y), ROWS), :],
                    s2_recv.at[u, d - 1],
                    send_sem.at[6],
                    s2_sem.at[k, u],
                    at_y(d),
                )
        else:
            wait_for(s1_recv.at[u, pl.ds(0, (Y - 1) * ROWS), :], s1_sem.at[k, u])
            total = s1_send[u, piece(y, ROWS), :].astype(F32)
            for d in range(1, Y):
                total = total + s1_recv[u, (d - 1) * ROWS : d * ROWS, :].astype(F32)
            for xq in range(X):
                s2_send[u, xq * ROWS : (xq + 1) * ROWS, :] = total[:, xq * span : (xq + 1) * span].astype(BF16)
            for d in range(1, X):
                send(
                    s2_send.at[u, piece(lax.rem(x + d, X), ROWS), :],
                    s2_recv.at[u, d - 1],
                    send_sem.at[6],
                    s2_sem.at[k, u],
                    at_x(d),
                )

    def plane_sum(k, u):
        n = Y if u % 2 == 0 else X
        wait_for(s2_recv.at[u, pl.ds(0, n - 1)], s2_sem.at[k, u])
        total = s2_send[u, piece(y if u % 2 == 0 else x, ROWS), :].astype(F32)
        for d in range(1, n):
            total = total + s2_recv[u, d - 1].astype(F32)
        return total

    def third_stage(k, u):
        total = plane_sum(k, u)
        if u:
            s3_send[u - 1] = total.astype(BF16)
            send(s3_send.at[u - 1], z_recv.at[k, u - 1], send_sem.at[7], s3_sem.at[k], at_z(u))
        return total

    def reduce(k, pt):
        for u in far:
            first_stage(k, u, pt)
        gather_sent(k)
        for u in far:
            second_stage(k, u)
        for u in far:
            total = third_stage(k, u)
        s2_own[...] = total

    def rows_of_block(k):
        wait_for(z_recv.at[k], s3_sem.at[k])
        total = s2_own[...]
        for d in range(1, Z):
            total = total + z_recv[k, d - 1].astype(F32)
        return total

    def reduce_sent(k):
        wait_for(z_recv.at[k], send_sem.at[7])
        for u in range(Z):
            if u % 2 == 0:
                wait_for(s1_recv.at[u, :, pl.ds(0, (X - 1) * span)], send_sem.at[5])
                wait_for(s2_recv.at[u, pl.ds(0, Y - 1)], send_sem.at[6])
            else:
                wait_for(s1_recv.at[u, pl.ds(0, (Y - 1) * ROWS), :], send_sem.at[5])
                wait_for(s2_recv.at[u, pl.ds(0, X - 1)], send_sem.at[6])

    row = lax.broadcasted_iota(jnp.int32, (count, count), 0)
    col = lax.broadcasted_iota(jnp.int32, (count, count), 1)
    eye = jnp.where(row == col, F32(1.0), F32(0.0))

    def weigh(gram, gvv, lower, diagonal):
        weights = jnp.where(lower, gram, F32(0.0))
        align = jnp.sum(diagonal * gram - weights * gvv, axis=1, keepdims=True)
        return diagonal * (F32(1.0) - F32(step_size) * align) - F32(step_size) * weights

    along_z(0)
    lax.fori_loop(0, Z * X, swap, 0)
    gather(0)
    proj, (gvv,) = whole(0)
    coef = [eye]
    wait_for(players_recv, send_sem.at[0])
    wait_for(data_v.at[pl.ds(0, depth)], swap_send_sem)

    for k in range(STEPS - 1):
        pt = (proj.astype(BF16).astype(F32) * F32(1.0 / nrows)).astype(BF16)
        reduce(k, pt)
        basis[k + 1, 0, piece(y, ROWS), piece(x, span)] = rows_of_block(k).astype(BF16)
        along_z(k + 1)
        gather(k + 1)
        q, inner = whole(k + 1)
        gram = exact(inner[0], coef[0], ((1,), (1,)))
        for b in range(1, k + 1):
            gram = gram + exact(inner[b], coef[b], ((1,), (1,)))
        mix = weigh(gram, gvv, col < row, eye)
        mixed = exact(mix, gvv)
        length = jnp.sum(
            mixed * mix + F32(2 * step_size) * mix * gram + F32(step_size**2) * eye * inner[k + 1],
            axis=1,
            keepdims=True,
        )
        scale = lax.rsqrt(length + F32(epsilon))
        proj = scale * (exact(mix, proj) + F32(step_size) * q)
        cross = exact(mix, gram, ((1,), (1,)))
        guu = (
            exact(mixed, mix, ((1,), (1,)))
            + F32(step_size) * (cross + cross.T)
            + F32(step_size**2) * inner[k + 1]
        )
        gvv = scale * guu * jnp.sum(eye * scale, axis=0, keepdims=True)
        coef = [scale * exact(mix, a) for a in coef] + [scale * F32(step_size) * eye]
        reduce_sent(k)

    k = STEPS - 1
    pt = (proj.astype(BF16).astype(F32) * F32(1.0 / nrows)).astype(BF16)
    gram = exact(pt.astype(F32), proj, ((1,), (1,)))
    gram_send[0] = jnp.concatenate([gram, jnp.zeros((count, 128 - count), F32)], axis=1)
    for d in range(1, Y):
        send(
            gram_send.at[0, piece(lax.rem(y + d, Y), ROWS), :],
            gram_recv.at[0, d - 1],
            send_sem.at[8],
            gram_sem.at[0],
            at_y(d),
        )
    for u in far:
        first_stage(k, u, pt)
    gather_sent(k)
    wait_for(gram_recv.at[0, pl.ds(0, Y - 1)], gram_sem.at[0])
    total = gram_send[0, piece(y, ROWS), :]
    for d in range(1, Y):
        total = total + gram_recv[0, d - 1]
    gram_send[1, :ROWS, :] = total
    for d in range(1, X):
        send(
            gram_send.at[1, pl.ds(0, ROWS)], gram_recv.at[1, d - 1], send_sem.at[9], gram_sem.at[1], at_x(d)
        )
    for u in far:
        second_stage(k, u)
    wait_for(gram_recv.at[1, pl.ds(0, X - 1)], gram_sem.at[1])
    total = gram_send[1, :ROWS, :]
    for d in range(1, X):
        total = total + gram_recv[1, d - 1]
    gram_send[2, :ROWS, :] = total
    for d in range(1, Z):
        send(
            gram_send.at[2, pl.ds(0, ROWS)], gram_z_recv.at[d - 1], send_sem.at[10], gram_sem.at[2], at_z(d)
        )
    for u in far:
        total = third_stage(k, u)
    s2_own[...] = total
    v = jnp.zeros((count, LANES), F32)
    for b in range(STEPS):
        v = v + exact(coef[b], basis[b, 0, :, piece(x, span)].astype(F32))
    gvv_v[...] = gvv
    row = lax.broadcasted_iota(jnp.int32, (ROWS, count), 0) + y * ROWS
    col = lax.broadcasted_iota(jnp.int32, (ROWS, count), 1)
    wait_for(gram_z_recv, gram_sem.at[2])
    total = gram_send[2, :ROWS, :]
    for d in range(1, Z):
        total = total + gram_z_recv[d - 1]
    mix = weigh(
        total[:, :count], gvv_v[piece(y, ROWS), :], col < row, jnp.where(row == col, F32(1.0), F32(0.0))
    )
    upd = exact(mix, v)
    upd = upd + F32(step_size) * rows_of_block(k)
    upd_v[...] = upd
    send(upd_v.at[piece(o, HALF), :], upd_recv, send_sem.at[0], upd_sem, sibling)
    sq_send[0] = jnp.broadcast_to(jnp.sum(upd * upd, axis=1, keepdims=True), (ROWS, 128))
    for d in range(1, Z):
        send(sq_send.at[0], sq_z_recv.at[d - 1], send_sem.at[1], sq_sem.at[0], at_z(d))
    wait_for(sq_z_recv, sq_sem.at[0])
    total = sq_send[0]
    for d in range(1, Z):
        total = total + sq_z_recv[d - 1]
    sq_send[1] = total
    for d in range(1, X):
        send(sq_send.at[1], sq_recv.at[d - 1], send_sem.at[2], sq_sem.at[1], at_x(d))
    wait_for(sq_recv, sq_sem.at[1])
    total = sq_send[1]
    for d in range(1, X):
        total = total + sq_recv[d - 1]
    sq_send[2] = total
    send(sq_send.at[2], sq_core_recv, send_sem.at[3], sq_sem.at[2], sibling)
    wait_for(sq_core_recv, sq_sem.at[2])
    wait_for(upd_recv, upd_sem)
    length = (sq_send[2, piece(c, HALF), :] + sq_core_recv[piece(c, HALF), :])[:, :1]
    scale = lax.rsqrt(length + F32(epsilon)) * F32((Z * X * 2 * LANES) ** 0.5)
    out_ref[:, piece(c, LANES)] = upd_v[piece(c, HALF), :] * scale
    out_ref[:, piece(o, LANES)] = upd_recv[...] * scale

    reduce_sent(k)
    wait_for(gram_recv.at[0, pl.ds(0, Y - 1)], send_sem.at[8])
    wait_for(gram_recv.at[1, pl.ds(0, X - 1)], send_sem.at[9])
    wait_for(gram_z_recv, send_sem.at[10])
    wait_for(upd_recv, send_sem.at[0])
    wait_for(sq_z_recv, send_sem.at[1])
    wait_for(sq_recv, send_sem.at[2])
    wait_for(sq_core_recv, send_sem.at[3])


def on_device(data, players):
    Z = lax.axis_size("wide") // X
    depth, features = data.shape
    nrows = depth * lax.axis_size("wide") * lax.axis_size("narrow")
    count = Y * ROWS
    span = LANES
    most = max(X, Y) - 1
    parts = 2 * depth + STEPS * count
    parts = -(-parts // 128) * 128
    dma = pltpu.SemaphoreType.DMA
    flops = STEPS * 4 * count * features * depth
    return pl.pallas_call(
        functools.partial(kernel, Z, nrows),
        out_shape=jax.ShapeDtypeStruct(players.shape, F32),
        in_specs=[pl.BlockSpec(memory_space=pl.ANY), pl.BlockSpec(memory_space=pltpu.VMEM)],
        out_specs=pl.BlockSpec(memory_space=pltpu.VMEM),
        scratch_shapes=[
            pltpu.VMEM((2 * depth, features // 2), BF16),
            pltpu.VMEM((STEPS, Z, count, X * span), BF16),
            pltpu.VMEM((HALF, LANES), F32),
            pltpu.VMEM((STEPS, count, parts), F32),
            pltpu.VMEM((STEPS, count, parts), F32),
            pltpu.VMEM((Z, count, X * span), BF16),
            pltpu.VMEM((Z, count, X * span), BF16),
            pltpu.VMEM((Z, max(X, Y) * ROWS, span), BF16),
            pltpu.VMEM((Z, most, ROWS, span), BF16),
            pltpu.VMEM((ROWS, span), F32),
            pltpu.VMEM((Z - 1, ROWS, span), BF16),
            pltpu.VMEM((STEPS, Z - 1, ROWS, span), BF16),
            pltpu.VMEM((3, count, 128), F32),
            pltpu.VMEM((2, most, ROWS, 128), F32),
            pltpu.VMEM((Z - 1, ROWS, 128), F32),
            pltpu.VMEM((3, ROWS, 128), F32),
            pltpu.VMEM((X - 1, ROWS, 128), F32),
            pltpu.VMEM((Z - 1, ROWS, 128), F32),
            pltpu.VMEM((ROWS, 128), F32),
            pltpu.VMEM((ROWS, LANES), F32),
            pltpu.VMEM((HALF, LANES), F32),
            pltpu.VMEM((count, count), F32),
            dma,
            dma,
            dma,
            dma((11,)),
            dma,
            dma((STEPS,)),
            dma((STEPS, Z)),
            dma((STEPS, Z)),
            dma((STEPS, Z)),
            dma((STEPS,)),
            dma((STEPS, Z)),
            dma((STEPS, Z)),
            dma((3,)),
            dma((3,)),
            dma,
        ],
        compiler_params=pltpu.CompilerParams(
            collective_id=0, has_side_effects=True, vmem_limit_bytes=52 * 2**20
        ),
        cost_estimate=pl.CostEstimate(flops=flops, bytes_accessed=2 * depth * features, transcendentals=0),
    )(data, players)


def solution(mesh):
    placed = (P(("wide", "narrow"), None), P("narrow", "wide"))
    return jax.shard_map(
        on_device, mesh=mesh, in_specs=placed, out_specs=P("narrow", "wide"), check_vma=False
    )
```

```python
import functools

import jax
import jax.numpy as jnp
from jax import lax
from jax.experimental import pallas as pl
from jax.experimental.pallas import tpu as pltpu
from jax.sharding import PartitionSpec as P

STEPS = 3
step_size = 0.5
epsilon = 1e-06

X = 4
Y = 4
ROWS = 16
HALF = ROWS // 2
LANES = 256

MESH = pl.DeviceIdType.MESH
F32 = jnp.float32
BF16 = jnp.bfloat16


def exact(a, b, contract=((1,), (0,))):
    return lax.dot_general(
        a, b, (contract, ((), ())), precision=lax.Precision.HIGHEST, preferred_element_type=F32
    )


def nt(a, b):
    return lax.dot_general(a, b, (((1,), (1,)), ((), ())), preferred_element_type=F32)


def order(n):
    return sorted(range(1, n), key=lambda d: -min(d, n - d))


def kernel(
    Z,
    nrows,
    data_hbm,
    players_ref,
    out_ref,
    data_v,
    basis,
    players_recv,
    part_send,
    part_recv,
    s1_send,
    s1_recv,
    s2_send,
    s2_recv,
    s2_own,
    s3_send,
    z_recv,
    gram_send,
    gram_recv,
    gram_z_recv,
    sq_send,
    sq_recv,
    sq_z_recv,
    sq_core_recv,
    upd_v,
    upd_recv,
    gvv_v,
    load_sem,
    swap_send_sem,
    swap_recv_sem,
    send_sem,
    first_sem,
    part_sem,
    za_sem,
    s1_sem,
    s2_sem,
    s3_sem,
    s4_sem,
    s5_sem,
    gram_sem,
    sq_sem,
    upd_sem,
):
    wide = lax.axis_index("wide")
    narrow = lax.axis_index("narrow")
    z, x = wide // X, wide % X
    y, c = narrow // 2, narrow % 2
    o = 1 - c
    count = Y * ROWS
    span = LANES
    unit = X * span
    near = sorted(range(Z), key=lambda d: (min(d, Z - d), d))
    far = near[::-1]
    depth = data_hbm.shape[0]

    def at_x(d):
        return (z * X + lax.rem(x + d, X), narrow)

    def at_y(d):
        return (wide, lax.rem(y + d, Y) * 2 + c)

    def at_z(d):
        return (lax.rem(z + d, Z) * X + x, narrow)

    sibling = (wide, y * 2 + o)

    def piece(at, size):
        return pl.ds(pl.multiple_of(at * size, size), size)

    def send(src, dst, ssem, rsem, where):
        pltpu.make_async_remote_copy(
            src_ref=src, dst_ref=dst, send_sem=ssem, recv_sem=rsem, device_id=where, device_id_type=MESH
        ).start()

    def wait_for(ref, sem):
        pltpu.make_async_copy(ref, ref, sem).wait()

    def place(q):
        return piece(c, depth), piece(lax.rem(q // X - z + Z, Z) * X + lax.rem(q, X), LANES)

    def load(q, carry):
        pltpu.make_async_copy(data_hbm.at[:, piece(q * 2 + c, LANES)], data_v.at[place(q)], load_sem).start()
        return carry


    barrier = pltpu.get_barrier_semaphore()
    peers = [at_z(d) for d in far[:-1]]
    peers += [at_x(d) for d in range(1, X)]
    peers += [at_y(d) for d in range(1, Y)]
    peers += [sibling]
    for peer in peers:
        pl.semaphore_signal(barrier, inc=1, device_id=peer, device_id_type=MESH)
    pl.semaphore_wait(barrier, len(peers))

    send(players_ref.at[:, piece(o, LANES)], players_recv, send_sem.at[0], first_sem, sibling)

    wait_for(players_recv, first_sem)
    mine = players_ref[:, piece(c, LANES)]
    theirs = players_recv[...]
    basis[0, 0, piece(y, ROWS), piece(x, span)] = jnp.where(
        c == 0, jnp.concatenate([mine, theirs], axis=0), jnp.concatenate([theirs, mine], axis=0)
    ).astype(BF16)

    def along_z(j):
        for d in near[1:]:
            send(
                basis.at[j, 0, piece(y, ROWS), piece(x, span)],
                basis.at[j, Z - d, piece(y, ROWS), piece(x, span)],
                send_sem.at[1],
                za_sem.at[j, Z - d],
                at_z(d),
            )

    def swap(q, carry):
        send(
            data_hbm.at[:, piece(q * 2 + o, LANES)],
            data_v.at[place(q)],
            swap_send_sem,
            swap_recv_sem,
            sibling,
        )
        return carry

    def fourth(j, u):
        if u:
            wait_for(z_recv.at[0, 0], za_sem.at[j, u])
        part = basis.at[j, u, piece(y, ROWS), piece(x, span)]
        if u % 2 == 0:
            for d in order(Y):
                send(part, part, send_sem.at[2], s4_sem.at[j, u], at_y(d))
        else:
            for d in order(X):
                send(part, part, send_sem.at[2], s4_sem.at[j, u], at_x(d))

    def fifth(j, u):
        if u % 2 == 0:
            wait_for(s2_recv.at[u, pl.ds(0, Y - 1)], s4_sem.at[j, u])
            part = basis.at[j, u, :, piece(x, span)]
            for d in order(X):
                send(part, part, send_sem.at[3], s5_sem.at[j, u], at_x(d))
        else:
            wait_for(s2_recv.at[u, pl.ds(0, X - 1)], s4_sem.at[j, u])
            part = basis.at[j, u, piece(y, ROWS), :]
            for d in order(Y):
                send(part, part, send_sem.at[3], s5_sem.at[j, u], at_y(d))

    def contract(j, u):
        if u % 2 == 0:
            wait_for(basis.at[j, u, :, pl.ds(0, (X - 1) * span)], s5_sem.at[j, u])
        else:
            wait_for(basis.at[j, u, pl.ds(0, (Y - 1) * ROWS), :], s5_sem.at[j, u])
        if j == 0 and u == near[0]:
            wait_for(data_v.at[pl.ds(0, depth)], load_sem)
            wait_for(data_v.at[pl.ds(0, depth)], swap_recv_sem)
        left = basis[j, u]
        q = nt(left, data_v[:, u * unit : (u + 1) * unit])
        g = jnp.concatenate([nt(left, basis[b, u]) for b in range(j + 1)], axis=1)
        if u == near[0]:
            part_send[j, :, : 2 * depth] = q
            part_send[j, :, 2 * depth : 2 * depth + (j + 1) * count] = g
        else:
            part_send[j, :, : 2 * depth] += q
            part_send[j, :, 2 * depth : 2 * depth + (j + 1) * count] += g

    def whole(j):
        part = part_send.at[j]
        send(part, part_recv.at[j], send_sem.at[4], part_sem.at[j], sibling)
        wait_for(part, part_sem.at[j])
        total = part_send[j, :, : 2 * depth + (j + 1) * count] + part_recv[j, :, : 2 * depth + (j + 1) * count]
        return total[:, : 2 * depth], [
            total[:, 2 * depth + b * count : 2 * depth + (b + 1) * count] for b in range(j + 1)
        ]

    def gather(j):
        fourth(j, 0)
        if j == 0:
            lax.fori_loop(0, Z * X, swap, 0)
        for u in near[1:3]:
            fourth(j, u)
        fifth(j, 0)
        if j == 0:
            lax.fori_loop(0, Z * X, load, 0)
        for u in near[3:]:
            fourth(j, u)
        for u in near[1:]:
            fifth(j, u)
        for u in near:
            contract(j, u)

    def gather_sent(j):
        wait_for(z_recv.at[0], send_sem.at[1])
        for u in range(Z):
            peers4, peers5 = (Y - 1, X - 1) if u % 2 == 0 else (X - 1, Y - 1)
            wait_for(s2_recv.at[u, pl.ds(0, peers4)], send_sem.at[2])
            if u % 2 == 0:
                wait_for(basis.at[j, u, :, pl.ds(0, (X - 1) * span)], send_sem.at[3])
            else:
                wait_for(basis.at[j, u, pl.ds(0, (Y - 1) * ROWS), :], send_sem.at[3])
        wait_for(part_send.at[j], send_sem.at[4])

    def first_stage(k, u, pt):
        for xq in range(X):
            at = u * unit + xq * span
            r = jnp.dot(pt, data_v[:, at : at + span], preferred_element_type=F32)
            s1_send[u, :, xq * span : (xq + 1) * span] = r.astype(BF16)
        if u % 2 == 0:
            for d in order(X):
                send(
                    s1_send.at[u, :, piece(lax.rem(x + d, X), span)],
                    s1_recv.at[u, :, pl.ds((d - 1) * span, span)],
                    send_sem.at[5],
                    s1_sem.at[k, u],
                    at_x(d),
                )
        else:
            for d in order(Y):
                send(
                    s1_send.at[u, piece(lax.rem(y + d, Y), ROWS), :],
                    s1_recv.at[u, pl.ds((d - 1) * ROWS, ROWS), :],
                    send_sem.at[5],
                    s1_sem.at[k, u],
                    at_y(d),
                )

    def second_stage(k, u):
        if u % 2 == 0:
            wait_for(s1_recv.at[u, :, pl.ds(0, (X - 1) * span)], s1_sem.at[k, u])
            total = s1_send[u, :, piece(x, span)].astype(F32)
            for d in range(1, X):
                total = total + s1_recv[u, :, (d - 1) * span : d * span].astype(F32)
            s2_send[u] = total.astype(BF16)
            for d in order(Y):
                send(
                    s2_send.at[u, piece(lax.rem(y + d, Y), ROWS), :],
                    s2_recv.at[u, d - 1],
                    send_sem.at[6],
                    s2_sem.at[k, u],
                    at_y(d),
                )
        else:
            wait_for(s1_recv.at[u, pl.ds(0, (Y - 1) * ROWS), :], s1_sem.at[k, u])
            total = s1_send[u, piece(y, ROWS), :].astype(F32)
            for d in range(1, Y):
                total = total + s1_recv[u, (d - 1) * ROWS : d * ROWS, :].astype(F32)
            for xq in range(X):
                s2_send[u, xq * ROWS : (xq + 1) * ROWS, :] = total[:, xq * span : (xq + 1) * span].astype(BF16)
            for d in order(X):
                send(
                    s2_send.at[u, piece(lax.rem(x + d, X), ROWS), :],
                    s2_recv.at[u, d - 1],
                    send_sem.at[6],
                    s2_sem.at[k, u],
                    at_x(d),
                )

    def plane_sum(k, u):
        n = Y if u % 2 == 0 else X
        wait_for(s2_recv.at[u, pl.ds(0, n - 1)], s2_sem.at[k, u])
        total = s2_send[u, piece(y if u % 2 == 0 else x, ROWS), :].astype(F32)
        for d in range(1, n):
            total = total + s2_recv[u, d - 1].astype(F32)
        return total

    def third_stage(k, u):
        total = plane_sum(k, u)
        if u:
            s3_send[u - 1] = total.astype(BF16)
            send(s3_send.at[u - 1], z_recv.at[k, u - 1], send_sem.at[7], s3_sem.at[k], at_z(u))
        return total

    def reduce(k, pt, meanwhile):
        for u in far:
            first_stage(k, u, pt)
        meanwhile()
        gather_sent(k)
        for u in far:
            second_stage(k, u)
        for u in far:
            total = third_stage(k, u)
        s2_own[...] = total

    def rows_of_block(k):
        wait_for(z_recv.at[k], s3_sem.at[k])
        total = s2_own[...]
        for d in range(1, Z):
            total = total + z_recv[k, d - 1].astype(F32)
        return total

    def reduce_sent(k):
        wait_for(z_recv.at[k], send_sem.at[7])
        for u in range(Z):
            if u % 2 == 0:
                wait_for(s1_recv.at[u, :, pl.ds(0, (X - 1) * span)], send_sem.at[5])
                wait_for(s2_recv.at[u, pl.ds(0, Y - 1)], send_sem.at[6])
            else:
                wait_for(s1_recv.at[u, pl.ds(0, (Y - 1) * ROWS), :], send_sem.at[5])
                wait_for(s2_recv.at[u, pl.ds(0, X - 1)], send_sem.at[6])

    row = lax.broadcasted_iota(jnp.int32, (count, count), 0)
    col = lax.broadcasted_iota(jnp.int32, (count, count), 1)
    eye = jnp.where(row == col, F32(1.0), F32(0.0))

    def weigh(gram, gvv, lower, diagonal):
        weights = jnp.where(lower, gram, F32(0.0))
        align = jnp.sum(diagonal * gram - weights * gvv, axis=1, keepdims=True)
        return diagonal * (F32(1.0) - F32(step_size) * align) - F32(step_size) * weights

    along_z(0)
    gather(0)
    proj, (gvv,) = whole(0)
    state = {"gvv": gvv, "coef": [eye]}

    def meanwhile():
        pass

    wait_for(players_recv, send_sem.at[0])
    wait_for(data_v.at[pl.ds(0, depth)], swap_send_sem)

    for k in range(STEPS - 1):
        pt = (proj.astype(BF16).astype(F32) * F32(1.0 / nrows)).astype(BF16)
        reduce(k, pt, meanwhile)
        basis[k + 1, 0, piece(y, ROWS), piece(x, span)] = rows_of_block(k).astype(BF16)
        along_z(k + 1)
        gather(k + 1)
        q, inner = whole(k + 1)
        gvv, coef = state["gvv"], state["coef"]
        gram = exact(inner[0], coef[0], ((1,), (1,)))
        for b in range(1, k + 1):
            gram = gram + exact(inner[b], coef[b], ((1,), (1,)))
        mix = weigh(gram, gvv, col < row, eye)
        mixed = exact(mix, gvv)
        length = jnp.sum(
            mixed * mix + F32(2 * step_size) * mix * gram + F32(step_size**2) * eye * inner[k + 1],
            axis=1,
            keepdims=True,
        )
        scale = lax.rsqrt(length + F32(epsilon))
        proj = scale * (exact(mix, proj) + F32(step_size) * q)

        def meanwhile(k=k, coef=coef, mix=mix, mixed=mixed, gram=gram, scale=scale, inner=inner):
            cross = exact(mix, gram, ((1,), (1,)))
            guu = (
                exact(mixed, mix, ((1,), (1,)))
                + F32(step_size) * (cross + cross.T)
                + F32(step_size**2) * inner[k + 1]
            )
            state["gvv"] = scale * guu * jnp.sum(eye * scale, axis=0, keepdims=True)
            state["coef"] = [scale * exact(mix, a) for a in coef] + [scale * F32(step_size) * eye]

        reduce_sent(k)

    k = STEPS - 1
    pt = (proj.astype(BF16).astype(F32) * F32(1.0 / nrows)).astype(BF16)
    gram = exact(pt.astype(F32), proj, ((1,), (1,)))
    gram_send[0] = jnp.concatenate([gram, jnp.zeros((count, 128 - count), F32)], axis=1)
    for d in order(Y):
        send(
            gram_send.at[0, piece(lax.rem(y + d, Y), ROWS), :],
            gram_recv.at[0, d - 1],
            send_sem.at[8],
            gram_sem.at[0],
            at_y(d),
        )
    for u in far:
        first_stage(k, u, pt)
    meanwhile()
    gvv, coef = state["gvv"], state["coef"]
    gather_sent(k)
    wait_for(gram_recv.at[0, pl.ds(0, Y - 1)], gram_sem.at[0])
    total = gram_send[0, piece(y, ROWS), :]
    for d in range(1, Y):
        total = total + gram_recv[0, d - 1]
    gram_send[1, :ROWS, :] = total
    for d in order(X):
        send(
            gram_send.at[1, pl.ds(0, ROWS)], gram_recv.at[1, d - 1], send_sem.at[9], gram_sem.at[1], at_x(d)
        )
    for u in far:
        second_stage(k, u)
    wait_for(gram_recv.at[1, pl.ds(0, X - 1)], gram_sem.at[1])
    total = gram_send[1, :ROWS, :]
    for d in range(1, X):
        total = total + gram_recv[1, d - 1]
    gram_send[2, :ROWS, :] = total
    for d in range(1, Z):
        send(
            gram_send.at[2, pl.ds(0, ROWS)], gram_z_recv.at[d - 1], send_sem.at[10], gram_sem.at[2], at_z(d)
        )
    for u in far:
        total = third_stage(k, u)
    s2_own[...] = total
    v = jnp.zeros((count, LANES), F32)
    for b in range(STEPS):
        v = v + exact(coef[b], basis[b, 0, :, piece(x, span)].astype(F32))
    gvv_v[...] = gvv
    row = lax.broadcasted_iota(jnp.int32, (ROWS, count), 0) + y * ROWS
    col = lax.broadcasted_iota(jnp.int32, (ROWS, count), 1)
    wait_for(gram_z_recv, gram_sem.at[2])
    total = gram_send[2, :ROWS, :]
    for d in range(1, Z):
        total = total + gram_z_recv[d - 1]
    mix = weigh(
        total[:, :count], gvv_v[piece(y, ROWS), :], col < row, jnp.where(row == col, F32(1.0), F32(0.0))
    )
    upd = exact(mix, v)
    upd = upd + F32(step_size) * rows_of_block(k)
    upd_v[...] = upd
    send(upd_v.at[piece(o, HALF), :], upd_recv, send_sem.at[0], upd_sem, sibling)
    sq_send[0] = jnp.broadcast_to(jnp.sum(upd * upd, axis=1, keepdims=True), (ROWS, 128))
    for d in range(1, Z):
        send(sq_send.at[0], sq_z_recv.at[d - 1], send_sem.at[1], sq_sem.at[0], at_z(d))
    wait_for(sq_z_recv, sq_sem.at[0])
    total = sq_send[0]
    for d in range(1, Z):
        total = total + sq_z_recv[d - 1]
    sq_send[1] = total
    for d in order(X):
        send(sq_send.at[1], sq_recv.at[d - 1], send_sem.at[2], sq_sem.at[1], at_x(d))
    wait_for(sq_recv, sq_sem.at[1])
    total = sq_send[1]
    for d in range(1, X):
        total = total + sq_recv[d - 1]
    sq_send[2] = total
    send(sq_send.at[2], sq_core_recv, send_sem.at[3], sq_sem.at[2], sibling)
    wait_for(sq_core_recv, sq_sem.at[2])
    wait_for(upd_recv, upd_sem)
    length = (sq_send[2, piece(c, HALF), :] + sq_core_recv[piece(c, HALF), :])[:, :1]
    scale = lax.rsqrt(length + F32(epsilon)) * F32((Z * X * 2 * LANES) ** 0.5)
    out_ref[:, piece(c, LANES)] = upd_v[piece(c, HALF), :] * scale
    out_ref[:, piece(o, LANES)] = upd_recv[...] * scale

    reduce_sent(k)
    wait_for(gram_recv.at[0, pl.ds(0, Y - 1)], send_sem.at[8])
    wait_for(gram_recv.at[1, pl.ds(0, X - 1)], send_sem.at[9])
    wait_for(gram_z_recv, send_sem.at[10])
    wait_for(upd_recv, send_sem.at[0])
    wait_for(sq_z_recv, send_sem.at[1])
    wait_for(sq_recv, send_sem.at[2])
    wait_for(sq_core_recv, send_sem.at[3])


def on_device(data, players):
    Z = lax.axis_size("wide") // X
    depth, features = data.shape
    nrows = depth * lax.axis_size("wide") * lax.axis_size("narrow")
    count = Y * ROWS
    span = LANES
    most = max(X, Y) - 1
    parts = 2 * depth + STEPS * count
    parts = -(-parts // 128) * 128
    dma = pltpu.SemaphoreType.DMA
    flops = STEPS * 4 * count * features * depth
    return pl.pallas_call(
        functools.partial(kernel, Z, nrows),
        out_shape=jax.ShapeDtypeStruct(players.shape, F32),
        in_specs=[pl.BlockSpec(memory_space=pl.ANY), pl.BlockSpec(memory_space=pltpu.VMEM)],
        out_specs=pl.BlockSpec(memory_space=pltpu.VMEM),
        scratch_shapes=[
            pltpu.VMEM((2 * depth, features // 2), BF16),
            pltpu.VMEM((STEPS, Z, count, X * span), BF16),
            pltpu.VMEM((HALF, LANES), F32),
            pltpu.VMEM((STEPS, count, parts), F32),
            pltpu.VMEM((STEPS, count, parts), F32),
            pltpu.VMEM((Z, count, X * span), BF16),
            pltpu.VMEM((Z, count, X * span), BF16),
            pltpu.VMEM((Z, max(X, Y) * ROWS, span), BF16),
            pltpu.VMEM((Z, most, ROWS, span), BF16),
            pltpu.VMEM((ROWS, span), F32),
            pltpu.VMEM((Z - 1, ROWS, span), BF16),
            pltpu.VMEM((STEPS, Z - 1, ROWS, span), BF16),
            pltpu.VMEM((3, count, 128), F32),
            pltpu.VMEM((2, most, ROWS, 128), F32),
            pltpu.VMEM((Z - 1, ROWS, 128), F32),
            pltpu.VMEM((3, ROWS, 128), F32),
            pltpu.VMEM((X - 1, ROWS, 128), F32),
            pltpu.VMEM((Z - 1, ROWS, 128), F32),
            pltpu.VMEM((ROWS, 128), F32),
            pltpu.VMEM((ROWS, LANES), F32),
            pltpu.VMEM((HALF, LANES), F32),
            pltpu.VMEM((count, count), F32),
            dma,
            dma,
            dma,
            dma((11,)),
            dma,
            dma((STEPS,)),
            dma((STEPS, Z)),
            dma((STEPS, Z)),
            dma((STEPS, Z)),
            dma((STEPS,)),
            dma((STEPS, Z)),
            dma((STEPS, Z)),
            dma((3,)),
            dma((3,)),
            dma,
        ],
        compiler_params=pltpu.CompilerParams(
            collective_id=0, has_side_effects=True, vmem_limit_bytes=52 * 2**20
        ),
        cost_estimate=pl.CostEstimate(flops=flops, bytes_accessed=2 * depth * features, transcendentals=0),
    )(data, players)


def solution(mesh):
    placed = (P(("wide", "narrow"), None), P("narrow", "wide"))
    return jax.shard_map(
        on_device, mesh=mesh, in_specs=placed, out_specs=P("narrow", "wide"), check_vma=False
    )
```
